128 devices in a mesh: chan: 16 (over z, x_lo, core), bin: 8 (over y, x_hi).
Axes of the slice: x: 4 (x_hi: 2, x_lo: 2; x = x_hi * 2 + x_lo), y: 4, z: 4, core: 2. Of those that a mesh axis runs over, the one named last changes fastest.
Arguments:
- records: bfloat16 [4096, 128, 2048], P('chan', 'bin'), may hold values from -6 to 6
- live_traces: int32 [4096], P('chan'), may hold values 0 or 1
- round_offsets: int32 [2], replicated, may hold values from 1 to 15, as said below
Outputs:
- cross_spectra: bfloat16 [3, 64, 2, 4096, 256], P(None, 'bin', None, 'chan')
The draws below stay inside these ranges and needn't reach their ends.
Inputs may be any that keep to these rules, and one draw needn't show every extreme that they name: `round_offsets`: the two offsets differ, and one of them is 15.
All inputs are finite; a program needn't handle non-finite values. No bound on the sum of `live_traces` on one device may be relied on, other than what follows from the above.
Results may differ from the reference program's by a relative error of at most 0.0077.
Values may be sent and summed in bfloat16 or wider, within the bound.
No kernel may reach another device: no remote copies, remote signals or barrier semaphores. Data moves between devices by JAX's collectives and lax.ppermute only.
A program may use at most 128 MiB of HBM per device.

```python
import math
import jax
import jax.numpy as jnp
from jax import lax

CH_DEV = 256
SAMPLES = 2048
BINS = 64
BAND_LO = 64
PAIRS = 3
CHANNELS = 4096
WINDOWS = 128
N_CHAN = 16


def draw_round_offsets(key, part):
    first_key = jax.random.fold_in(key, 11)
    second_key = jax.random.fold_in(key, 23)
    position = jax.random.randint(first_key, (1,), 0, 2)
    other = jax.random.randint(second_key, (1,), 1, N_CHAN - 1)
    farthest = jnp.full((1,), N_CHAN - 1, jnp.int32)
    leading = jnp.where(position == 0, farthest, other)
    trailing = jnp.where(position == 0, other, farthest)
    return jnp.concatenate([leading, trailing]).astype(jnp.int32)


def touch_ends(values, stream_key, smallest, top_value):
    spot = [jax.random.randint(jax.random.fold_in(stream_key, axis), (), 0, length) for axis, length in enumerate(values.shape)]
    widest = values.shape.index(max(values.shape))
    neighbour = spot[:widest] + [(spot[widest] + 1) % values.shape[widest]] + spot[widest + 1:]
    return values.at[tuple(spot)].set(smallest).at[tuple(neighbour)].set(top_value)


def block_levels(stream_key, shape, cuts, least, high):
    gain = 1.0
    for axis_at, shards_of in cuts:
        steps = jax.random.uniform(jax.random.fold_in(jax.random.fold_in(stream_key, 6), axis_at), (shards_of,), jnp.float32, least / len(cuts), high / len(cuts))
        gain = gain * jnp.repeat(jnp.exp(steps), shape[axis_at] // shards_of).reshape((-1,) + (1,) * (len(shape) - 1 - axis_at))
    return gain


def bell_draw(stream_key, extent, deviation, bound, pieces=(), held_as=jnp.bfloat16):
    drawn = deviation * jax.random.normal(stream_key, extent, jnp.float32)
    if pieces:
        drawn = drawn * block_levels(stream_key, extent, pieces, -0.22, 0.18)
    return jnp.clip(drawn, -bound, bound).astype(held_as)


def setup_inputs(seed: int = 0) -> dict:
    key_of = jax.random.split(jax.random.key(seed), 4)
    records = bell_draw(key_of[0], (CHANNELS, WINDOWS, SAMPLES), 1.0, 6.0, ((0, 16), (1, 8)))
    live_traces = touch_ends((jax.random.randint(key_of[1], (CHANNELS,), 0, 10) < 9).astype(jnp.int32), jax.random.fold_in(key_of[1], 1), 0, 1)
    round_offsets = draw_round_offsets(jax.random.fold_in(key_of[3], 71), 0)
    return {"records": records, "live_traces": live_traces, "round_offsets": round_offsets}


eps = 1e-06

def dft_table(length, first_bin, bins):
    samples = jnp.arange(length, dtype=jnp.int32)
    freqs = first_bin + jnp.arange(bins, dtype=jnp.int32)
    phase = samples[:, None] * freqs[None, :] % length
    angle = phase.astype(jnp.float32) * (2.0 * math.pi / length)
    both = jnp.stack([jnp.cos(angle), -jnp.sin(angle)], axis=-1) / math.sqrt(length)
    return both.reshape(length, 2 * bins).astype(jnp.bfloat16)

def whiten(block, live):
    values = block.astype(jnp.float32)
    power = lax.optimization_barrier(jnp.mean(values * values, axis=-1, keepdims=True))
    keep = live.astype(jnp.float32)[:, None, None]
    return (values * lax.rsqrt(power + eps) * keep).astype(jnp.bfloat16)

def cross(mine, other, scale):
    product = jnp.einsum('fpwi,fqwj->fpqij', mine.astype(jnp.float32), other.astype(jnp.float32))
    real_part = product[:, 0, 0] + product[:, 1, 1]
    imag_part = product[:, 0, 1] - product[:, 1, 0]
    return (jnp.stack([real_part, imag_part], axis=1) * scale).astype(jnp.bfloat16)

def reference(records, live_traces, round_offsets):
    table = dft_table(SAMPLES, BAND_LO, BINS)
    blocks = records.reshape(N_CHAN, CH_DEV, WINDOWS, SAMPLES)
    masks = live_traces.reshape(N_CHAN, CH_DEV)

    def transform(item):
        block, live = item
        whitened = whiten(block, live)
        spectrum = jnp.einsum('cws,sq->qwc', whitened.astype(jnp.float32), table.astype(jnp.float32))
        return spectrum.astype(jnp.bfloat16)
    spectra = lax.map(transform, (blocks, masks))
    spectra = spectra.reshape(N_CHAN, BINS, 2, WINDOWS, CH_DEV)
    offsets = jnp.concatenate([jnp.zeros((1,), jnp.int32), round_offsets.astype(jnp.int32)])
    scale = 1.0 / math.sqrt(WINDOWS)

    def pair_block(index):
        mine = spectra[index]
        results = []
        for pair in range(PAIRS):
            partner = (index + offsets[pair]) % N_CHAN
            results.append(cross(mine, spectra[partner], scale))
        return jnp.stack(results)
    stacked = lax.map(pair_block, jnp.arange(N_CHAN, dtype=jnp.int32))
    stacked = jnp.transpose(stacked, (1, 2, 3, 0, 4, 5))
    return stacked.reshape(PAIRS, BINS, 2, CHANNELS, CH_DEV)
```

```python
import functools
import math

import numpy as np
import jax
import jax.numpy as jnp
from jax import lax
from jax.experimental import pallas as pl
from jax.experimental.pallas import tpu as pltpu
from jax.sharding import PartitionSpec as P

SAMPLES = 2048
BINS = 64
BAND_LO = 64
WINDOWS = 128
N_CHAN = 16
N_Y = 4
EPS = 1e-06

BLOCK = 256
HALF = 128
STEP = 16
W_DEV = 16
F_DEV = 8
LIMIT = 56 * 1024 * 1024


def dft_table():
    samples = np.arange(SAMPLES, dtype=np.int64)
    freqs = BAND_LO + np.arange(BINS, dtype=np.int64)
    phase = samples[:, None] * freqs[None, :] % SAMPLES
    angle = phase.astype(np.float64) * (2.0 * math.pi / SAMPLES)
    both = np.stack([np.cos(angle), -np.sin(angle)], axis=-1) / math.sqrt(SAMPLES)
    return both.reshape(SAMPLES, 2 * BINS).astype(np.float32).astype(jnp.bfloat16)


def transform_kernel(pos_ref, x_ref, t_ref, live_ref, *refs):
    outs, (s1, s2) = refs[:N_Y], refs[N_Y:]
    i = pl.program_id(0)
    rows = STEP * W_DEV
    x = x_ref[...].reshape(rows, SAMPLES)
    res = jnp.dot(x, t_ref[...], preferred_element_type=jnp.float32)
    acc = None
    for j in range(SAMPLES // 128):
        part = x[:, j * 128:(j + 1) * 128].astype(jnp.float32)
        acc = part * part if acc is None else acc + part * part
    power = jnp.sum(acc, axis=-1, keepdims=True) * (1.0 / SAMPLES)
    s1[pl.ds(pl.multiple_of(i * rows, rows), rows), :] = res * lax.rsqrt(power + EPS)

    @pl.when(i == pl.num_programs(0) - 1)
    def _():
        keep = live_ref[...].astype(jnp.float32)
        for w in range(W_DEV):
            plane = s1[pl.ds(w, HALF, stride=W_DEV), :]
            s2[pl.ds(w, 2 * BINS, stride=W_DEV), :] = plane.T * keep
        y, xh = pos_ref[0], pos_ref[1]
        size = F_DEV * 2 * W_DEV
        for dy in range(N_Y):
            for dx in range(2):
                group = ((y + dy) % N_Y) * 2 + (xh + dx) % 2
                piece = s2[pl.ds(pl.multiple_of(group * size, size), size), :]
                outs[dy][dx] = piece.astype(jnp.bfloat16).reshape(F_DEV, 2 * W_DEV, HALF)


def transform(pos, records, table, live, part):
    steps = HALF // STEP
    piece = jax.ShapeDtypeStruct((2, F_DEV, 2 * W_DEV, HALF), jnp.bfloat16)
    return pl.pallas_call(
        transform_kernel,
        out_shape=[piece] * N_Y,
        grid_spec=pltpu.PrefetchScalarGridSpec(
            num_scalar_prefetch=1,
            grid=(steps,),
            in_specs=[
                pl.BlockSpec((STEP, W_DEV, SAMPLES), lambda i, pos: (part * steps + i, 0, 0)),
                pl.BlockSpec((SAMPLES, 2 * BINS), lambda i, pos: (0, 0)),
                pl.BlockSpec((1, HALF), lambda i, pos: (0, part)),
            ],
            out_specs=[pl.BlockSpec(piece.shape, lambda i, pos: (0, 0, 0, 0))] * N_Y,
            scratch_shapes=[
                pltpu.VMEM((HALF * W_DEV, 2 * BINS), jnp.float32),
                pltpu.VMEM((2 * BINS * W_DEV, HALF), jnp.float32),
            ],
        ),
        compiler_params=pltpu.CompilerParams(vmem_limit_bytes=LIMIT),
        cost_estimate=pl.CostEstimate(
            flops=2 * HALF * W_DEV * SAMPLES * 2 * BINS,
            bytes_accessed=HALF * W_DEV * SAMPLES * 2,
            transcendentals=0,
        ),
        name="transform",
    )(pos, records, table, live)


K_HALF = N_Y * 2 * W_DEV
K_ALL = 2 * K_HALF
SCALE = 1.0 / math.sqrt(WINDOWS)


def rows_of(same, other):
    return jnp.concatenate(
        [same[...].reshape(K_HALF, HALF), other[...].reshape(K_HALF, HALF)], axis=0
    )


def own_kernel(m0, o0, m1, o1, out_ref, left_ref):
    mine = jnp.concatenate([rows_of(m0, o0), rows_of(m1, o1)], axis=1)
    split = mine.reshape(2 * N_Y, 2, W_DEV, BLOCK)
    turned = jnp.concatenate([-split[:, 1:], split[:, :1]], axis=1).reshape(K_ALL, BLOCK)
    left = jnp.concatenate([mine.T, turned.T], axis=0)
    left_ref[0] = left
    both = jnp.dot(left, mine, preferred_element_type=jnp.float32) * SCALE
    out_ref[0, 0] = both.reshape(2, BLOCK, BLOCK).astype(jnp.bfloat16)


OUT = jax.ShapeDtypeStruct((3, F_DEV, 2, BLOCK, BLOCK), jnp.bfloat16)
PIECE_SPEC = (N_Y, 1, 2 * W_DEV, HALF)


def own_pair(pieces):
    spec = pl.BlockSpec(PIECE_SPEC, lambda f: (0, f, 0, 0))
    return pl.pallas_call(
        own_kernel,
        out_shape=[OUT, jax.ShapeDtypeStruct((F_DEV, 2 * BLOCK, K_ALL), jnp.bfloat16)],
        grid=(F_DEV,),
        in_specs=[spec] * 4,
        out_specs=[
            pl.BlockSpec((1, 1, 2, BLOCK, BLOCK), lambda f: (0, f, 0, 0, 0)),
            pl.BlockSpec((1, 2 * BLOCK, K_ALL), lambda f: (f, 0, 0)),
        ],
        compiler_params=pltpu.CompilerParams(vmem_limit_bytes=LIMIT),
        cost_estimate=pl.CostEstimate(
            flops=2 * F_DEV * 2 * BLOCK * K_ALL * BLOCK, bytes_accessed=6 << 20, transcendentals=0
        ),
        name="own_pair",
    )(*pieces)


def round_kernel(q_ref, left_ref, same, other, _, out_ref):
    theirs = rows_of(same, other)
    both = jnp.dot(left_ref[0], theirs, preferred_element_type=jnp.float32) * SCALE
    out_ref[0, 0] = both.reshape(2, BLOCK, HALF).astype(jnp.bfloat16)


def round_pair(pairing, left, same, other, out, part):
    spec = pl.BlockSpec(PIECE_SPEC, lambda f, q: (0, f, 0, 0))
    return pl.pallas_call(
        round_kernel,
        out_shape=OUT,
        grid_spec=pltpu.PrefetchScalarGridSpec(
            num_scalar_prefetch=1,
            grid=(F_DEV,),
            in_specs=[
                pl.BlockSpec((1, 2 * BLOCK, K_ALL), lambda f, q: (f, 0, 0)),
                spec,
                spec,
                pl.BlockSpec(memory_space=pl.ANY),
            ],
            out_specs=pl.BlockSpec(
                (1, 1, 2, BLOCK, HALF), lambda f, q: (q[0], f, 0, 0, part)
            ),
        ),
        input_output_aliases={4: 0},
        compiler_params=pltpu.CompilerParams(vmem_limit_bytes=LIMIT),
        cost_estimate=pl.CostEstimate(
            flops=2 * F_DEV * 2 * BLOCK * K_ALL * HALF, bytes_accessed=4 << 20, transcendentals=0
        ),
        name="round_pair",
    )(pairing, left, same, other, out)


def along_y(value, dy):
    pairs = [
        (y * 2 + h, (y + dy) % N_Y * 2 + h) for y in range(N_Y) for h in range(2)
    ]
    return lax.ppermute(value, "bin", pairs)


def towards(value, offset, flip):
    n_bin = 2 * N_Y
    pairs = []
    for a in range(N_CHAN):
        for g in range(n_bin):
            source = (a + offset) % N_CHAN * n_bin + (g ^ flip)
            pairs.append((source, a * n_bin + g))
    return lax.ppermute(value, ("chan", "bin"), pairs)


def y_stage(pieces):
    got = [pieces[0]] + [along_y(pieces[dy], dy) for dy in range(1, N_Y)]
    same = jnp.stack([piece[0] for piece in got])
    other = jnp.stack([piece[1] for piece in got])
    return same, other


def body(records, live_traces, round_offsets):
    table = jnp.asarray(dft_table())
    live = live_traces.reshape(1, BLOCK)
    g = lax.axis_index("bin").astype(jnp.int32)
    pos = jnp.stack([g // 2, g % 2])
    first = round_offsets[0]
    last_first = first == N_CHAN - 1
    k = jnp.where(last_first, round_offsets[1], first)
    q15 = jnp.where(last_first, 1, 2).astype(jnp.int32).reshape(1)
    qk = 3 - q15

    parts = [transform(pos, records, table, live, h) for h in range(2)]
    firsts = y_stage(parts[0])

    def rest(offset, firsts, second, q15, qk):
        sent = [firsts]
        sent.append(y_stage(second))
        swapped, near, far = [], [], []
        for same, other in sent:
            swapped.append(towards(other, 0, 1))
            near.append((towards(same, 15, 0), towards(other, 15, 1)))
            far.append((towards(same, offset, 0), towards(other, offset, 1)))
        out, left = own_pair([sent[0][0], swapped[0], sent[1][0], swapped[1]])
        for h in range(2):
            out = round_pair(q15, left, *near[h], out, h)
            out = round_pair(qk, left, *far[h], out, h)
        return out

    branches = [functools.partial(rest, offset) for offset in range(1, N_CHAN - 1)]
    return lax.switch(k - 1, branches, firsts, parts[1], q15, qk)


def solution(mesh):
    in_specs = (P("chan", "bin", None), P("chan"), P())
    out_specs = P(None, "bin", None, "chan", None)
    return jax.shard_map(body, mesh=mesh, in_specs=in_specs, out_specs=out_specs, check_vma=False)
```

```python
import functools
import math

import numpy as np
import jax
import jax.numpy as jnp
from jax import lax
from jax.experimental import pallas as pl
from jax.experimental.pallas import tpu as pltpu
from jax.sharding import PartitionSpec as P

SAMPLES = 2048
BINS = 64
BAND_LO = 64
WINDOWS = 128
N_CHAN = 16
N_Y = 4
EPS = 1e-06

BLOCK = 256
LANES = 128
STEP = 32
W_DEV = 16
F_DEV = 8
PAIRS = 3
LIMIT = 60 * 1024 * 1024
SCALE = 1.0 / math.sqrt(WINDOWS)


def dft_table():
    samples = np.arange(SAMPLES, dtype=np.int64)
    freqs = BAND_LO + np.arange(BINS, dtype=np.int64)
    phase = samples[:, None] * freqs[None, :] % SAMPLES
    angle = phase.astype(np.float64) * (2.0 * math.pi / SAMPLES)
    both = np.stack([np.cos(angle), -np.sin(angle)], axis=-1) / math.sqrt(SAMPLES)
    return both.reshape(SAMPLES, 2 * BINS).astype(np.float32).astype(jnp.bfloat16)


def transform_kernel(x_hbm, t_hbm, live_ref, *refs):
    outs, (xb, table, s1, s2, sems) = refs[:2 * N_Y], refs[2 * N_Y:]
    steps = BLOCK // STEP
    rows = STEP * W_DEV

    def load(b):
        at = pl.ds(b * STEP, STEP)
        return pltpu.make_async_copy(x_hbm.at[at], xb.at[at], sems.at[b])

    load_table = pltpu.make_async_copy(t_hbm, table, sems.at[steps])
    load_table.start()
    for b in range(steps):
        load(b).start()
    load_table.wait()

    def step(b, carry):
        load(b).wait()
        x = xb[pl.ds(b * STEP, STEP)].reshape(rows, SAMPLES)
        res = jnp.dot(x, table[...], preferred_element_type=jnp.float32)
        acc = None
        for j in range(SAMPLES // LANES):
            part = x[:, j * LANES:(j + 1) * LANES].astype(jnp.float32)
            acc = part * part if acc is None else acc + part * part
        power = jnp.sum(acc, axis=-1, keepdims=True) * (1.0 / SAMPLES)
        s1[pl.ds(pl.multiple_of(b * rows, rows), rows), :] = res * lax.rsqrt(power + EPS)
        return carry

    lax.fori_loop(0, steps, step, 0)
    for h in range(BLOCK // LANES):
        keep = live_ref[:, h * LANES:(h + 1) * LANES].astype(jnp.float32)
        for w in range(W_DEV):
            plane = s1[pl.ds(h * LANES * W_DEV + w, LANES, stride=W_DEV), :]
            s2[pl.ds(h * 2 * BINS * W_DEV + w, 2 * BINS, stride=W_DEV), :] = plane.T * keep
    g = lax.axis_index("bin")
    y, xh = g // 2, g % 2
    size = F_DEV * 2 * W_DEV
    for h in range(BLOCK // LANES):
        for dx in range(2):
            for dy in range(N_Y):
                group = ((y + dy) % N_Y) * 2 + (xh + dx) % 2
                start = h * 2 * BINS * W_DEV + group * size
                piece = s2[pl.ds(pl.multiple_of(start, size), size), :]
                outs[dx * N_Y + dy][:, :, h * LANES:(h + 1) * LANES] = (
                    piece.astype(jnp.bfloat16).reshape(F_DEV, 2 * W_DEV, LANES)
                )


def transform(records, table, live):
    piece = jax.ShapeDtypeStruct((F_DEV, 2 * W_DEV, BLOCK), jnp.bfloat16)
    vmem = pl.BlockSpec(memory_space=pltpu.VMEM)
    hbm = pl.BlockSpec(memory_space=pltpu.HBM)
    return pl.pallas_call(
        transform_kernel,
        out_shape=[piece] * (2 * N_Y),
        in_specs=[hbm, hbm, vmem],
        out_specs=[vmem] * (2 * N_Y),
        scratch_shapes=[
            pltpu.VMEM((BLOCK, W_DEV, SAMPLES), jnp.bfloat16),
            pltpu.VMEM((SAMPLES, 2 * BINS), jnp.bfloat16),
            pltpu.VMEM((BLOCK * W_DEV, 2 * BINS), jnp.float32),
            pltpu.VMEM((BLOCK // LANES * 2 * BINS * W_DEV, LANES), jnp.float32),
            pltpu.SemaphoreType.DMA((BLOCK // STEP + 1,)),
        ],
        compiler_params=pltpu.CompilerParams(vmem_limit_bytes=LIMIT),
        cost_estimate=pl.CostEstimate(
            flops=2 * BLOCK * W_DEV * SAMPLES * 2 * BINS,
            bytes_accessed=BLOCK * W_DEV * SAMPLES * 2,
            transcendentals=0,
        ),
        name="transform",
    )(records, table, live)


K_HALF = N_Y * 2 * W_DEV
K_ALL = 2 * K_HALF


def rows_of(pair, f):
    return jnp.concatenate(
        [half[:, pl.ds(f, 1)].reshape(K_HALF, BLOCK) for half in pair], axis=0
    )


def cross_kernel(q_ref, *refs):
    halves, out_hbm, stage, sems = refs[:6], refs[6], refs[7], refs[8]
    own, near, far = halves[:2], halves[2:4], halves[4:]

    def store(p, f):
        pairing = 0 if p == 0 else q_ref[p - 1]
        return pltpu.make_async_copy(stage.at[p, f], out_hbm.at[pairing, f], sems.at[p, f])

    def step(f, carry):
        mine = rows_of(own, f)
        split = mine.reshape(2 * N_Y, 2, W_DEV, BLOCK)
        turned = jnp.concatenate([-split[:, 1:], split[:, :1]], axis=1)
        left = jnp.concatenate([mine.T, turned.reshape(K_ALL, BLOCK).T], axis=0)
        for p, theirs in enumerate((mine, rows_of(near, f), rows_of(far, f))):
            both = jnp.dot(left, theirs, preferred_element_type=jnp.float32) * SCALE
            stage[p, f] = both.reshape(2, BLOCK, BLOCK).astype(jnp.bfloat16)
            store(p, f).start()
        return carry

    lax.fori_loop(0, F_DEV, step, 0)

    def finish(f, carry):
        for p in range(PAIRS):
            store(p, f).wait()
        return carry

    lax.fori_loop(0, F_DEV, finish, 0)


def cross(pairings, halves):
    return pl.pallas_call(
        cross_kernel,
        out_shape=jax.ShapeDtypeStruct((PAIRS, F_DEV, 2, BLOCK, BLOCK), jnp.bfloat16),
        in_specs=[pl.BlockSpec(memory_space=pltpu.SMEM)]
        + [pl.BlockSpec(memory_space=pltpu.VMEM)] * 6,
        out_specs=pl.BlockSpec(memory_space=pl.ANY),
        scratch_shapes=[
            pltpu.VMEM((PAIRS, F_DEV, 2, BLOCK, BLOCK), jnp.bfloat16),
            pltpu.SemaphoreType.DMA((PAIRS, F_DEV)),
        ],
        compiler_params=pltpu.CompilerParams(vmem_limit_bytes=16 << 20),
        cost_estimate=pl.CostEstimate(
            flops=2 * PAIRS * F_DEV * 2 * BLOCK * K_ALL * BLOCK,
            bytes_accessed=10 << 20,
            transcendentals=0,
        ),
        name="cross",
    )(pairings, *halves)


def along_y(value, dy):
    pairs = [
        (y * 2 + h, (y + dy) % N_Y * 2 + h) for y in range(N_Y) for h in range(2)
    ]
    return lax.ppermute(value, "bin", pairs)


def towards(value, offset, flip):
    n_bin = 2 * N_Y
    pairs = []
    for a in range(N_CHAN):
        for g in range(n_bin):
            source = (a + offset) % N_CHAN * n_bin + (g ^ flip)
            pairs.append((source, a * n_bin + g))
    return lax.ppermute(value, ("chan", "bin"), pairs)


def y_stage(pieces):
    return jnp.stack([pieces[0]] + [along_y(pieces[dy], dy) for dy in range(1, N_Y)])


def far_pair(k, same, other):
    return towards(same, k, 0), towards(other, k, 1)


def body(records, live_traces, round_offsets):
    table = jnp.asarray(dft_table())
    live = live_traces.reshape(1, BLOCK)
    first = round_offsets[0]
    last_first = first == N_CHAN - 1
    k = jnp.where(last_first, round_offsets[1], first)
    q_near = jnp.where(last_first, 1, 2).astype(jnp.int32)
    pairings = jnp.stack([q_near, 3 - q_near])

    pieces = transform(records, table, live)
    other = y_stage(pieces[N_Y:])
    same = y_stage(pieces[:N_Y])
    swapped = towards(other, 0, 1)
    near_other = towards(other, N_CHAN - 1, 1)
    near_same = towards(same, N_CHAN - 1, 0)
    branches = [functools.partial(far_pair, offset) for offset in range(1, N_CHAN - 1)]
    far_same, far_other = lax.switch(k - 1, branches, same, other)
    return cross(pairings, (same, swapped, near_same, near_other, far_same, far_other))


def solution(mesh):
    in_specs = (P("chan", "bin", None), P("chan"), P())
    out_specs = P(None, "bin", None, "chan", None)
    return jax.shard_map(body, mesh=mesh, in_specs=in_specs, out_specs=out_specs, check_vma=False)
```

```python
import functools
import math

import numpy as np
import jax
import jax.numpy as jnp
from jax import lax
from jax.experimental import pallas as pl
from jax.experimental.pallas import tpu as pltpu
from jax.sharding import PartitionSpec as P

SAMPLES = 2048
BINS = 64
BAND_LO = 64
WINDOWS = 128
N_CHAN = 16
N_BIN = 8
EPS = 1e-06

BLOCK = 256
LANES = 128
STEP = 32
W_DEV = 16
F_DEV = 8
F_PART = 4
PARTS = F_DEV // F_PART
PAIRS = 3
LIMIT = 60 * 1024 * 1024
SCALE = 1.0 / math.sqrt(WINDOWS)


def dft_table():
    samples = np.arange(SAMPLES, dtype=np.int64)
    freqs = BAND_LO + np.arange(BINS, dtype=np.int64)
    phase = samples[:, None] * freqs[None, :] % SAMPLES
    angle = phase.astype(np.float64) * (2.0 * math.pi / SAMPLES)
    both = np.stack([np.cos(angle), -np.sin(angle)], axis=-1) / math.sqrt(SAMPLES)
    return both.reshape(SAMPLES, 2 * BINS).astype(np.float32).astype(jnp.bfloat16)


def transform_kernel(x_hbm, t_hbm, live_ref, *refs):
    outs, (xb, table, s1, s2, sems) = refs[:PARTS], refs[PARTS:]
    steps = BLOCK // STEP
    rows = STEP * W_DEV

    def load(b):
        at = pl.ds(b * STEP, STEP)
        return pltpu.make_async_copy(x_hbm.at[at], xb.at[at], sems.at[b])

    load_table = pltpu.make_async_copy(t_hbm, table, sems.at[steps])
    load_table.start()
    for b in range(steps):
        load(b).start()
    load_table.wait()

    def step(b, carry):
        load(b).wait()
        x = xb[pl.ds(b * STEP, STEP)].reshape(rows, SAMPLES)
        res = jnp.dot(x, table[...], preferred_element_type=jnp.float32)
        acc = None
        for j in range(SAMPLES // LANES):
            part = x[:, j * LANES:(j + 1) * LANES].astype(jnp.float32)
            acc = part * part if acc is None else acc + part * part
        power = jnp.sum(acc, axis=-1, keepdims=True) * (1.0 / SAMPLES)
        s1[pl.ds(pl.multiple_of(b * rows, rows), rows), :] = res * lax.rsqrt(power + EPS)
        return carry

    lax.fori_loop(0, steps, step, 0)
    for h in range(BLOCK // LANES):
        keep = live_ref[:, h * LANES:(h + 1) * LANES].astype(jnp.float32)
        for w in range(W_DEV):
            plane = s1[pl.ds(h * LANES * W_DEV + w, LANES, stride=W_DEV), :]
            s2[pl.ds(h * 2 * BINS * W_DEV + w, 2 * BINS, stride=W_DEV), :] = plane.T * keep
    size = F_PART * 2 * W_DEV
    for h in range(BLOCK // LANES):
        for g in range(N_BIN):
            for c in range(PARTS):
                start = h * 2 * BINS * W_DEV + (g * PARTS + c) * size
                piece = s2[start:start + size, :].astype(jnp.bfloat16)
                outs[c][g, :, :, h * LANES:(h + 1) * LANES] = (
                    piece.reshape(F_PART, 2 * W_DEV, LANES)
                )


def transform(records, table, live):
    piece = jax.ShapeDtypeStruct((N_BIN, F_PART, 2 * W_DEV, BLOCK), jnp.bfloat16)
    vmem = pl.BlockSpec(memory_space=pltpu.VMEM)
    hbm = pl.BlockSpec(memory_space=pltpu.HBM)
    return pl.pallas_call(
        transform_kernel,
        out_shape=[piece] * PARTS,
        in_specs=[hbm, hbm, vmem],
        out_specs=[vmem] * PARTS,
        scratch_shapes=[
            pltpu.VMEM((BLOCK, W_DEV, SAMPLES), jnp.bfloat16),
            pltpu.VMEM((SAMPLES, 2 * BINS), jnp.bfloat16),
            pltpu.VMEM((BLOCK * W_DEV, 2 * BINS), jnp.float32),
            pltpu.VMEM((BLOCK // LANES * 2 * BINS * W_DEV, LANES), jnp.float32),
            pltpu.SemaphoreType.DMA((BLOCK // STEP + 1,)),
        ],
        compiler_params=pltpu.CompilerParams(vmem_limit_bytes=LIMIT),
        cost_estimate=pl.CostEstimate(
            flops=2 * BLOCK * W_DEV * SAMPLES * 2 * BINS,
            bytes_accessed=BLOCK * W_DEV * SAMPLES * 2,
            transcendentals=0,
        ),
        name="transform",
    )(records, table, live)


K_ALL = N_BIN * 2 * W_DEV
OUT = jax.ShapeDtypeStruct((PAIRS, F_DEV, 2, BLOCK, BLOCK), jnp.bfloat16)


def rows_of(part, f):
    return part[:, pl.ds(f, 1)].reshape(K_ALL, BLOCK)


def left_of(mine):
    split = mine.reshape(N_BIN, 2, W_DEV, BLOCK)
    turned = jnp.concatenate([-split[:, 1:], split[:, :1]], axis=1)
    return jnp.concatenate([mine.T, turned.reshape(K_ALL, BLOCK).T], axis=0)


def product(left, theirs):
    both = jnp.dot(left, theirs, preferred_element_type=jnp.float32) * SCALE
    return both.reshape(2, BLOCK, BLOCK).astype(jnp.bfloat16)


def store(stage, sems, out_hbm, slot, pairing, f):
    return pltpu.make_async_copy(stage.at[slot], out_hbm.at[pairing, f], sems.at[slot])


def first_kernel(q_ref, own1, own2, near1, far1, out_hbm, left_ref, stage, sems):
    def pairs(f, own, others):
        mine = rows_of(own, f % F_PART)
        left = left_of(mine)
        left_ref[f] = left
        for p, other in enumerate((None, *others)):
            theirs = mine if other is None else rows_of(other, f)
            slot = f if p == 0 else F_DEV + (p - 1) * F_PART + f
            stage[slot] = product(left, theirs)
            store(stage, sems, out_hbm, slot, 0 if p == 0 else q_ref[p - 1], f).start()

    def half1(f, carry):
        pairs(f, own1, (near1, far1))
        return carry

    def half2(f, carry):
        pairs(f, own2, ())
        return carry

    lax.fori_loop(0, F_PART, half1, 0)
    lax.fori_loop(F_PART, F_DEV, half2, 0)

    def finish(slot, carry):
        store(stage, sems, out_hbm, slot, 0, 0).wait()
        return carry

    lax.fori_loop(0, 2 * F_DEV, finish, 0)


def first_pairs(pairings, *parts):
    vmem = pl.BlockSpec(memory_space=pltpu.VMEM)
    return pl.pallas_call(
        first_kernel,
        out_shape=[OUT, jax.ShapeDtypeStruct((F_DEV, 2 * BLOCK, K_ALL), jnp.bfloat16)],
        in_specs=[pl.BlockSpec(memory_space=pltpu.SMEM)] + [vmem] * 4,
        out_specs=[pl.BlockSpec(memory_space=pl.ANY), vmem],
        scratch_shapes=[
            pltpu.VMEM((2 * F_DEV, 2, BLOCK, BLOCK), jnp.bfloat16),
            pltpu.SemaphoreType.DMA((2 * F_DEV,)),
        ],
        compiler_params=pltpu.CompilerParams(vmem_limit_bytes=16 << 20),
        cost_estimate=pl.CostEstimate(
            flops=2 * 2 * F_DEV * 2 * BLOCK * K_ALL * BLOCK,
            bytes_accessed=8 << 20,
            transcendentals=0,
        ),
        name="first_pairs",
    )(pairings, *parts)


def last_kernel(q_ref, left_ref, near2, far2, _, out_hbm, stage, sems):
    def step(f, carry):
        left = left_ref[F_PART + f]
        for p, other in enumerate((near2, far2)):
            slot = p * F_PART + f
            stage[slot] = product(left, rows_of(other, f))
            store(stage, sems, out_hbm, slot, q_ref[p], F_PART + f).start()
        return carry

    lax.fori_loop(0, F_PART, step, 0)

    def finish(slot, carry):
        store(stage, sems, out_hbm, slot, 0, 0).wait()
        return carry

    lax.fori_loop(0, 2 * F_PART, finish, 0)


def last_pairs(pairings, left, near2, far2, out):
    vmem = pl.BlockSpec(memory_space=pltpu.VMEM)
    hbm = pl.BlockSpec(memory_space=pl.ANY)
    return pl.pallas_call(
        last_kernel,
        out_shape=OUT,
        in_specs=[pl.BlockSpec(memory_space=pltpu.SMEM), vmem, vmem, vmem, hbm],
        out_specs=hbm,
        scratch_shapes=[
            pltpu.VMEM((2 * F_PART, 2, BLOCK, BLOCK), jnp.bfloat16),
            pltpu.SemaphoreType.DMA((2 * F_PART,)),
        ],
        input_output_aliases={4: 0},
        compiler_params=pltpu.CompilerParams(vmem_limit_bytes=12 << 20),
        cost_estimate=pl.CostEstimate(
            flops=2 * F_DEV * 2 * BLOCK * K_ALL * BLOCK, bytes_accessed=5 << 20, transcendentals=0
        ),
        name="last_pairs",
    )(pairings, left, near2, far2, out)


def towards(value, offset):
    return lax.ppermute(
        value, "chan", [((a + offset) % N_CHAN, a) for a in range(N_CHAN)]
    )


def regroup(value):
    return lax.all_to_all(value, "bin", split_axis=0, concat_axis=0, tiled=True)


def rounds(k, own1, raw2, pairings):
    far1 = towards(own1, k)
    own2 = regroup(raw2)
    near1 = towards(own1, N_CHAN - 1)
    far2 = towards(own2, k)
    near2 = towards(own2, N_CHAN - 1)
    out, left = first_pairs(pairings, own1, own2, near1, far1)
    return out, left, near2, far2


def body(records, live_traces, round_offsets):
    table = jnp.asarray(dft_table())
    live = live_traces.reshape(1, BLOCK)
    raw1, raw2, round_offsets = lax.optimization_barrier(
        (*transform(records, table, live), round_offsets)
    )
    first = round_offsets[0]
    last_first = first == N_CHAN - 1
    k = jnp.where(last_first, round_offsets[1], first)
    q_near = jnp.where(last_first, 1, 2).astype(jnp.int32)
    pairings = jnp.stack([q_near, 3 - q_near])
    own1, k, pairings = lax.optimization_barrier((regroup(raw1), k, pairings))
    branches = [functools.partial(rounds, offset) for offset in range(1, N_CHAN - 1)]
    out, left, near2, far2 = lax.switch(k - 1, branches, own1, raw2, pairings)
    return last_pairs(pairings, left, near2, far2, out)


def solution(mesh):
    in_specs = (P("chan", "bin", None), P("chan"), P())
    out_specs = P(None, "bin", None, "chan", None)
    return jax.shard_map(body, mesh=mesh, in_specs=in_specs, out_specs=out_specs, check_vma=False)
```

```python
import functools
import math

import numpy as np
import jax
import jax.numpy as jnp
from jax import lax
from jax.experimental import pallas as pl
from jax.experimental.pallas import tpu as pltpu
from jax.sharding import PartitionSpec as P

SAMPLES = 2048
BINS = 64
BAND_LO = 64
WINDOWS = 128
N_CHAN = 16
N_BIN = 8
EPS = 1e-06

BLOCK = 256
LANES = 128
STEP = 32
W_DEV = 16
F_DEV = 8
HALF = 128
PAIRS = 3
LIMIT = 60 * 1024 * 1024
SCALE = 1.0 / math.sqrt(WINDOWS)


def dft_table():
    samples = np.arange(SAMPLES, dtype=np.int64)
    freqs = BAND_LO + np.arange(BINS, dtype=np.int64)
    phase = samples[:, None] * freqs[None, :] % SAMPLES
    angle = phase.astype(np.float64) * (2.0 * math.pi / SAMPLES)
    both = np.stack([np.cos(angle), -np.sin(angle)], axis=-1) / math.sqrt(SAMPLES)
    return both.reshape(SAMPLES, 2 * BINS).astype(np.float32).astype(jnp.bfloat16)


def transform_kernel(part, x_hbm, t_hbm, live_ref, out_ref, xb, table, s1, s2, sems):
    steps = HALF // STEP
    rows = STEP * W_DEV

    def load(b):
        return pltpu.make_async_copy(
            x_hbm.at[pl.ds(part * HALF + b * STEP, STEP)],
            xb.at[pl.ds(b * STEP, STEP)],
            sems.at[b],
        )

    load_table = pltpu.make_async_copy(t_hbm, table, sems.at[steps])
    load_table.start()
    for b in range(steps):
        load(b).start()
    load_table.wait()

    def step(b, carry):
        load(b).wait()
        x = xb[pl.ds(b * STEP, STEP)].reshape(rows, SAMPLES)
        res = jnp.dot(x, table[...], preferred_element_type=jnp.float32)
        acc = None
        for j in range(SAMPLES // LANES):
            piece = x[:, j * LANES:(j + 1) * LANES].astype(jnp.float32)
            acc = piece * piece if acc is None else acc + piece * piece
        power = jnp.sum(acc, axis=-1, keepdims=True) * (1.0 / SAMPLES)
        s1[pl.ds(pl.multiple_of(b * rows, rows), rows), :] = res * lax.rsqrt(power + EPS)
        return carry

    lax.fori_loop(0, steps, step, 0)
    keep = live_ref[:, part * HALF:(part + 1) * HALF].astype(jnp.float32)
    for w in range(W_DEV):
        plane = s1[pl.ds(w, HALF, stride=W_DEV), :]
        s2[pl.ds(w, 2 * BINS, stride=W_DEV), :] = plane.T * keep
    size = F_DEV * 2 * W_DEV
    for g in range(N_BIN):
        piece = s2[g * size:(g + 1) * size, :].astype(jnp.bfloat16)
        out_ref[g] = piece.reshape(F_DEV, 2 * W_DEV, HALF)


def transform(records, table, live, part):
    vmem = pl.BlockSpec(memory_space=pltpu.VMEM)
    hbm = pl.BlockSpec(memory_space=pltpu.HBM)
    return pl.pallas_call(
        functools.partial(transform_kernel, part),
        out_shape=jax.ShapeDtypeStruct((N_BIN, F_DEV, 2 * W_DEV, HALF), jnp.bfloat16),
        in_specs=[hbm, hbm, vmem],
        out_specs=vmem,
        scratch_shapes=[
            pltpu.VMEM((HALF, W_DEV, SAMPLES), jnp.bfloat16),
            pltpu.VMEM((SAMPLES, 2 * BINS), jnp.bfloat16),
            pltpu.VMEM((HALF * W_DEV, 2 * BINS), jnp.float32),
            pltpu.VMEM((2 * BINS * W_DEV, HALF), jnp.float32),
            pltpu.SemaphoreType.DMA((HALF // STEP + 1,)),
        ],
        compiler_params=pltpu.CompilerParams(vmem_limit_bytes=LIMIT),
        cost_estimate=pl.CostEstimate(
            flops=2 * HALF * W_DEV * SAMPLES * 2 * BINS,
            bytes_accessed=HALF * W_DEV * SAMPLES * 2,
            transcendentals=0,
        ),
        name="transform",
    )(records, table, live)


K_ALL = N_BIN * 2 * W_DEV
OUT = jax.ShapeDtypeStruct((PAIRS, F_DEV, 2, BLOCK, BLOCK), jnp.bfloat16)


def rows_of(left, right, f):
    halves = [part[:, pl.ds(f, 1)].reshape(K_ALL, HALF) for part in (left, right)]
    return jnp.concatenate(halves, axis=1)


def left_of(mine):
    split = mine.reshape(N_BIN, 2, W_DEV, BLOCK)
    turned = jnp.concatenate([-split[:, 1:], split[:, :1]], axis=1)
    return jnp.concatenate([mine.T, turned.reshape(K_ALL, BLOCK).T], axis=0)


def product(left, theirs):
    both = jnp.dot(left, theirs, preferred_element_type=jnp.float32) * SCALE
    return both.reshape(2, BLOCK, BLOCK).astype(jnp.bfloat16)


def rounds_of(part, q_ref, left, near, far, out_hbm, stage, sems, f):
    stage[f] = product(left, rows_of(near, far, f))
    for copy in round_copies(part, q_ref, out_hbm, stage, sems, f):
        copy.start()


def round_copies(part, q_ref, out_hbm, stage, sems, f):
    columns = pl.ds(part * HALF, HALF)
    return [
        pltpu.make_async_copy(
            stage.at[f, :, :, pl.ds(n * HALF, HALF)],
            out_hbm.at[q_ref[n], f, :, :, columns],
            sems.at[n, f],
        )
        for n in range(2)
    ]


def first_kernel(q_ref, own1, own2, near, far, out_hbm, left_ref, own_stage, stage, own_sems, sems):
    def own_copy(f):
        return pltpu.make_async_copy(own_stage.at[f], out_hbm.at[0, f], own_sems.at[f])

    def step(f, carry):
        mine = rows_of(own1, own2, f)
        left = left_of(mine)
        left_ref[f] = left
        own_stage[f] = product(left, mine)
        own_copy(f).start()
        rounds_of(0, q_ref, left, near, far, out_hbm, stage, sems, f)
        return carry

    lax.fori_loop(0, F_DEV, step, 0)

    def finish(f, carry):
        own_copy(f).wait()
        for copy in round_copies(0, q_ref, out_hbm, stage, sems, f):
            copy.wait()
        return carry

    lax.fori_loop(0, F_DEV, finish, 0)


def first_pairs(pairings, *parts):
    vmem = pl.BlockSpec(memory_space=pltpu.VMEM)
    slots = pltpu.VMEM((F_DEV, 2, BLOCK, BLOCK), jnp.bfloat16)
    return pl.pallas_call(
        first_kernel,
        out_shape=[OUT, jax.ShapeDtypeStruct((F_DEV, 2 * BLOCK, K_ALL), jnp.bfloat16)],
        in_specs=[pl.BlockSpec(memory_space=pltpu.SMEM)] + [vmem] * 4,
        out_specs=[pl.BlockSpec(memory_space=pl.ANY), vmem],
        scratch_shapes=[
            slots,
            slots,
            pltpu.SemaphoreType.DMA((F_DEV,)),
            pltpu.SemaphoreType.DMA((2, F_DEV)),
        ],
        compiler_params=pltpu.CompilerParams(vmem_limit_bytes=16 << 20),
        cost_estimate=pl.CostEstimate(
            flops=2 * 2 * F_DEV * 2 * BLOCK * K_ALL * BLOCK,
            bytes_accessed=8 << 20,
            transcendentals=0,
        ),
        name="first_pairs",
    )(pairings, *parts)


def last_kernel(q_ref, left_ref, near, far, _, out_hbm, stage, sems):
    def step(f, carry):
        rounds_of(1, q_ref, left_ref[f], near, far, out_hbm, stage, sems, f)
        return carry

    lax.fori_loop(0, F_DEV, step, 0)

    def finish(f, carry):
        for copy in round_copies(1, q_ref, out_hbm, stage, sems, f):
            copy.wait()
        return carry

    lax.fori_loop(0, F_DEV, finish, 0)


def last_pairs(pairings, left, near, far, out):
    vmem = pl.BlockSpec(memory_space=pltpu.VMEM)
    hbm = pl.BlockSpec(memory_space=pl.ANY)
    return pl.pallas_call(
        last_kernel,
        out_shape=OUT,
        in_specs=[pl.BlockSpec(memory_space=pltpu.SMEM), vmem, vmem, vmem, hbm],
        out_specs=hbm,
        scratch_shapes=[
            pltpu.VMEM((F_DEV, 2, BLOCK, BLOCK), jnp.bfloat16),
            pltpu.SemaphoreType.DMA((2, F_DEV)),
        ],
        input_output_aliases={4: 0},
        compiler_params=pltpu.CompilerParams(vmem_limit_bytes=12 << 20),
        cost_estimate=pl.CostEstimate(
            flops=2 * F_DEV * 2 * BLOCK * K_ALL * BLOCK, bytes_accessed=5 << 20, transcendentals=0
        ),
        name="last_pairs",
    )(pairings, left, near, far, out)


def towards(value, offset):
    return lax.ppermute(
        value, "chan", [((a + offset) % N_CHAN, a) for a in range(N_CHAN)]
    )


def regroup(value):
    return lax.all_to_all(value, "bin", split_axis=0, concat_axis=0, tiled=True)


def rounds(k, own1, raw2, pairings):
    far1 = towards(own1, k)
    own2 = regroup(raw2)
    near1 = towards(own1, N_CHAN - 1)
    far2 = towards(own2, k)
    near2 = towards(own2, N_CHAN - 1)
    out, left = first_pairs(pairings, own1, own2, near1, far1)
    return last_pairs(pairings, left, near2, far2, out)


def body(records, live_traces, round_offsets):
    table = jnp.asarray(dft_table())
    live = live_traces.reshape(1, BLOCK)
    raw1, round_offsets = lax.optimization_barrier(
        (transform(records, table, live, 0), round_offsets)
    )
    raw2 = transform(records, table, live, 1)
    first = round_offsets[0]
    last_first = first == N_CHAN - 1
    k = jnp.where(last_first, round_offsets[1], first)
    q_near = jnp.where(last_first, 1, 2).astype(jnp.int32)
    pairings = jnp.stack([q_near, 3 - q_near])
    own1, k, pairings = lax.optimization_barrier((regroup(raw1), k, pairings))
    branches = [functools.partial(rounds, offset) for offset in range(1, N_CHAN - 1)]
    return lax.switch(k - 1, branches, own1, raw2, pairings)


def solution(mesh):
    in_specs = (P("chan", "bin", None), P("chan"), P())
    out_specs = P(None, "bin", None, "chan", None)
    return jax.shard_map(body, mesh=mesh, in_specs=in_specs, out_specs=out_specs, check_vma=False)
```

```python
import functools
import math

import numpy as np
import jax
import jax.numpy as jnp
from jax import lax
from jax.experimental import pallas as pl
from jax.experimental.pallas import tpu as pltpu
from jax.sharding import PartitionSpec as P

SAMPLES = 2048
BINS = 64
BAND_LO = 64
WINDOWS = 128
N_CHAN = 16
N_BIN = 8
EPS = 1e-06

BLOCK = 256
LANES = 128
STEP = 32
W_DEV = 16
F_DEV = 8
HALF = 128
PAIRS = 3
LIMIT = 60 * 1024 * 1024
SCALE = 1.0 / math.sqrt(WINDOWS)


def dft_table():
    samples = np.arange(SAMPLES, dtype=np.int64)
    freqs = BAND_LO + np.arange(BINS, dtype=np.int64)
    phase = samples[:, None] * freqs[None, :] % SAMPLES
    angle = phase.astype(np.float64) * (2.0 * math.pi / SAMPLES)
    both = np.stack([np.cos(angle), -np.sin(angle)], axis=-1) / math.sqrt(SAMPLES)
    return both.reshape(SAMPLES, 2 * BINS).astype(np.float32).astype(jnp.bfloat16)


def plan_kernel(offsets_ref, x_hbm, t_hbm, live_ref, out_ref, branch_ref, pairings_ref, *scratch):
    last_first = offsets_ref[0] == N_CHAN - 1
    branch_ref[0] = jnp.where(last_first, offsets_ref[1], offsets_ref[0]) - 1
    near = jnp.where(last_first, 1, 2)
    pairings_ref[0] = near
    pairings_ref[1] = PAIRS - near
    transform_kernel(0, x_hbm, t_hbm, live_ref, out_ref, *scratch)


def transform_kernel(part, x_hbm, t_hbm, live_ref, out_ref, xb, table, s1, s2, sems):
    steps = HALF // STEP
    rows = STEP * W_DEV

    def load(b):
        return pltpu.make_async_copy(
            x_hbm.at[pl.ds(part * HALF + b * STEP, STEP)],
            xb.at[pl.ds(b * STEP, STEP)],
            sems.at[b],
        )

    load_table = pltpu.make_async_copy(t_hbm, table, sems.at[steps])
    load_table.start()
    for b in range(steps):
        load(b).start()
    load_table.wait()

    def step(b, carry):
        load(b).wait()
        x = xb[pl.ds(b * STEP, STEP)].reshape(rows, SAMPLES)
        res = jnp.dot(x, table[...], preferred_element_type=jnp.float32)
        acc = None
        for j in range(SAMPLES // LANES):
            piece = x[:, j * LANES:(j + 1) * LANES].astype(jnp.float32)
            acc = piece * piece if acc is None else acc + piece * piece
        power = jnp.sum(acc, axis=-1, keepdims=True) * (1.0 / SAMPLES)
        s1[pl.ds(pl.multiple_of(b * rows, rows), rows), :] = res * lax.rsqrt(power + EPS)
        return carry

    lax.fori_loop(0, steps, step, 0)
    keep = live_ref[:, part * HALF:(part + 1) * HALF].astype(jnp.float32)
    for w in range(W_DEV):
        plane = s1[pl.ds(w, HALF, stride=W_DEV), :]
        s2[pl.ds(w, 2 * BINS, stride=W_DEV), :] = plane.T * keep
    size = F_DEV * 2 * W_DEV
    for g in range(N_BIN):
        piece = s2[g * size:(g + 1) * size, :].astype(jnp.bfloat16)
        out_ref[g] = piece.reshape(F_DEV, 2 * W_DEV, HALF)


def transform(records, table, live, offsets=None):
    vmem = pl.BlockSpec(memory_space=pltpu.VMEM)
    hbm = pl.BlockSpec(memory_space=pltpu.HBM)
    smem = pl.BlockSpec(memory_space=pltpu.SMEM)
    out_shape = jax.ShapeDtypeStruct((N_BIN, F_DEV, 2 * W_DEV, HALF), jnp.bfloat16)
    plan_shapes = [jax.ShapeDtypeStruct((n,), jnp.int32) for n in (1, 2)]
    extra = () if offsets is None else (offsets,)
    return pl.pallas_call(
        functools.partial(transform_kernel, 1) if offsets is None else plan_kernel,
        out_shape=out_shape if offsets is None else [out_shape, *plan_shapes],
        in_specs=[smem] * len(extra) + [hbm, hbm, vmem],
        out_specs=vmem if offsets is None else [vmem, smem, smem],
        scratch_shapes=[
            pltpu.VMEM((HALF, W_DEV, SAMPLES), jnp.bfloat16),
            pltpu.VMEM((SAMPLES, 2 * BINS), jnp.bfloat16),
            pltpu.VMEM((HALF * W_DEV, 2 * BINS), jnp.float32),
            pltpu.VMEM((2 * BINS * W_DEV, HALF), jnp.float32),
            pltpu.SemaphoreType.DMA((HALF // STEP + 1,)),
        ],
        compiler_params=pltpu.CompilerParams(vmem_limit_bytes=LIMIT),
        cost_estimate=pl.CostEstimate(
            flops=2 * HALF * W_DEV * SAMPLES * 2 * BINS,
            bytes_accessed=HALF * W_DEV * SAMPLES * 2,
            transcendentals=0,
        ),
        name="transform",
    )(*extra, records, table, live)


K_ALL = N_BIN * 2 * W_DEV
OUT = jax.ShapeDtypeStruct((PAIRS, F_DEV, 2, BLOCK, BLOCK), jnp.bfloat16)


def rows_of(left, right, f):
    halves = [part[:, pl.ds(f, 1)].reshape(K_ALL, HALF) for part in (left, right)]
    return jnp.concatenate(halves, axis=1)


def left_of(mine):
    split = mine.reshape(N_BIN, 2, W_DEV, BLOCK)
    turned = jnp.concatenate([-split[:, 1:], split[:, :1]], axis=1)
    return jnp.concatenate([mine.T, turned.reshape(K_ALL, BLOCK).T], axis=0)


def product(left, theirs):
    both = jnp.dot(left, theirs, preferred_element_type=jnp.float32) * SCALE
    return both.reshape(2, BLOCK, BLOCK).astype(jnp.bfloat16)


def rounds_of(part, q_ref, left, near, far, out_hbm, stage, sems, f):
    stage[f] = product(left, rows_of(near, far, f))
    for copy in round_copies(part, q_ref, out_hbm, stage, sems, f):
        copy.start()


def round_copies(part, q_ref, out_hbm, stage, sems, f):
    columns = pl.ds(part * HALF, HALF)
    return [
        pltpu.make_async_copy(
            stage.at[f, :, :, pl.ds(n * HALF, HALF)],
            out_hbm.at[q_ref[n], f, :, :, columns],
            sems.at[n, f],
        )
        for n in range(2)
    ]


def first_kernel(q_ref, own1, own2, near, far, out_hbm, left_ref, own_stage, stage, own_sems, sems):
    def own_copy(f):
        return pltpu.make_async_copy(own_stage.at[f], out_hbm.at[0, f], own_sems.at[f])

    def step(f, carry):
        mine = rows_of(own1, own2, f)
        left = left_of(mine)
        left_ref[f] = left
        own_stage[f] = product(left, mine)
        own_copy(f).start()
        rounds_of(0, q_ref, left, near, far, out_hbm, stage, sems, f)
        return carry

    lax.fori_loop(0, F_DEV, step, 0)

    def finish(f, carry):
        own_copy(f).wait()
        for copy in round_copies(0, q_ref, out_hbm, stage, sems, f):
            copy.wait()
        return carry

    lax.fori_loop(0, F_DEV, finish, 0)


def first_pairs(pairings, *parts):
    vmem = pl.BlockSpec(memory_space=pltpu.VMEM)
    slots = pltpu.VMEM((F_DEV, 2, BLOCK, BLOCK), jnp.bfloat16)
    return pl.pallas_call(
        first_kernel,
        out_shape=[OUT, jax.ShapeDtypeStruct((F_DEV, 2 * BLOCK, K_ALL), jnp.bfloat16)],
        in_specs=[pl.BlockSpec(memory_space=pltpu.SMEM)] + [vmem] * 4,
        out_specs=[pl.BlockSpec(memory_space=pl.ANY), vmem],
        scratch_shapes=[
            slots,
            slots,
            pltpu.SemaphoreType.DMA((F_DEV,)),
            pltpu.SemaphoreType.DMA((2, F_DEV)),
        ],
        compiler_params=pltpu.CompilerParams(vmem_limit_bytes=16 << 20),
        cost_estimate=pl.CostEstimate(
            flops=2 * 2 * F_DEV * 2 * BLOCK * K_ALL * BLOCK,
            bytes_accessed=8 << 20,
            transcendentals=0,
        ),
        name="first_pairs",
    )(pairings, *parts)


def last_kernel(q_ref, left_ref, near, far, _, out_hbm, stage, sems):
    def step(f, carry):
        rounds_of(1, q_ref, left_ref[f], near, far, out_hbm, stage, sems, f)
        return carry

    lax.fori_loop(0, F_DEV, step, 0)

    def finish(f, carry):
        for copy in round_copies(1, q_ref, out_hbm, stage, sems, f):
            copy.wait()
        return carry

    lax.fori_loop(0, F_DEV, finish, 0)


def last_pairs(pairings, left, near, far, out):
    vmem = pl.BlockSpec(memory_space=pltpu.VMEM)
    hbm = pl.BlockSpec(memory_space=pl.ANY)
    return pl.pallas_call(
        last_kernel,
        out_shape=OUT,
        in_specs=[pl.BlockSpec(memory_space=pltpu.SMEM), vmem, vmem, vmem, hbm],
        out_specs=hbm,
        scratch_shapes=[
            pltpu.VMEM((F_DEV, 2, BLOCK, BLOCK), jnp.bfloat16),
            pltpu.SemaphoreType.DMA((2, F_DEV)),
        ],
        input_output_aliases={4: 0},
        compiler_params=pltpu.CompilerParams(vmem_limit_bytes=12 << 20),
        cost_estimate=pl.CostEstimate(
            flops=2 * F_DEV * 2 * BLOCK * K_ALL * BLOCK, bytes_accessed=5 << 20, transcendentals=0
        ),
        name="last_pairs",
    )(pairings, left, near, far, out)


def towards(value, offset):
    return lax.ppermute(
        value, "chan", [((a + offset) % N_CHAN, a) for a in range(N_CHAN)]
    )


def regroup(value):
    return lax.all_to_all(value, "bin", split_axis=0, concat_axis=0, tiled=True)


def rounds(k, own1, raw2, pairings):
    far1 = towards(own1, k)
    own2 = regroup(raw2)
    near1 = towards(own1, N_CHAN - 1)
    far2 = towards(own2, k)
    near2 = towards(own2, N_CHAN - 1)
    out, left = first_pairs(pairings, own1, own2, near1, far1)
    return last_pairs(pairings, left, near2, far2, out)


def body(records, live_traces, round_offsets):
    table = jnp.asarray(dft_table())
    live = live_traces.reshape(1, BLOCK)
    raw1, branch, pairings = transform(records, table, live, round_offsets)
    raw2 = transform(records, table, live)
    own1 = regroup(raw1)
    branches = [functools.partial(rounds, offset) for offset in range(1, N_CHAN - 1)]
    return lax.switch(branch[0], branches, own1, raw2, pairings)


def solution(mesh):
    in_specs = (P("chan", "bin", None), P("chan"), P())
    out_specs = P(None, "bin", None, "chan", None)
    return jax.shard_map(body, mesh=mesh, in_specs=in_specs, out_specs=out_specs, check_vma=False)
```

```python
import functools
import math

import numpy as np
import jax
import jax.numpy as jnp
from jax import lax
from jax.experimental import pallas as pl
from jax.experimental.pallas import tpu as pltpu
from jax.sharding import PartitionSpec as P

SAMPLES = 2048
BINS = 64
BAND_LO = 64
WINDOWS = 128
N_CHAN = 16
N_BIN = 8
EPS = 1e-06

BLOCK = 256
LANES = 128
STEP = 32
W_DEV = 16
F_DEV = 8
HALF = 128
PAIRS = 3
LIMIT = 60 * 1024 * 1024
SCALE = 1.0 / math.sqrt(WINDOWS)


def dft_table():
    samples = np.arange(SAMPLES, dtype=np.int64)
    freqs = BAND_LO + np.arange(BINS, dtype=np.int64)
    phase = samples[:, None] * freqs[None, :] % SAMPLES
    angle = phase.astype(np.float64) * (2.0 * math.pi / SAMPLES)
    both = np.stack([np.cos(angle), -np.sin(angle)], axis=-1) / math.sqrt(SAMPLES)
    return both.reshape(SAMPLES, 2 * BINS).astype(np.float32).astype(jnp.bfloat16)


def plan_kernel(offsets_ref, x_hbm, t_hbm, live_ref, out_ref, branch_ref, pairings_ref, *scratch):
    last_first = offsets_ref[0] == N_CHAN - 1
    branch_ref[0] = jnp.where(last_first, offsets_ref[1], offsets_ref[0]) - 1
    near = jnp.where(last_first, 1, 2)
    pairings_ref[0] = near
    pairings_ref[1] = PAIRS - near
    transform_kernel(0, x_hbm, t_hbm, live_ref, out_ref, *scratch)


def transform_kernel(part, x_hbm, t_hbm, live_ref, out_ref, xb, table, s1, s2, sems):
    steps = HALF // STEP
    rows = STEP * W_DEV

    def load(b):
        return pltpu.make_async_copy(
            x_hbm.at[pl.ds(part * HALF + b * STEP, STEP)],
            xb.at[pl.ds(b * STEP, STEP)],
            sems.at[b],
        )

    load_table = pltpu.make_async_copy(t_hbm, table, sems.at[steps])
    load_table.start()
    for b in range(steps):
        load(b).start()
    load_table.wait()

    def step(b, carry):
        load(b).wait()
        x = xb[pl.ds(b * STEP, STEP)].reshape(rows, SAMPLES)
        res = jnp.dot(x, table[...], preferred_element_type=jnp.float32)
        acc = None
        for j in range(SAMPLES // LANES):
            piece = x[:, j * LANES:(j + 1) * LANES].astype(jnp.float32)
            acc = piece * piece if acc is None else acc + piece * piece
        power = jnp.sum(acc, axis=-1, keepdims=True) * (1.0 / SAMPLES)
        s1[pl.ds(pl.multiple_of(b * rows, rows), rows), :] = res * lax.rsqrt(power + EPS)
        return carry

    lax.fori_loop(0, steps, step, 0)
    keep = live_ref[:, part * HALF:(part + 1) * HALF].astype(jnp.float32)
    for w in range(W_DEV):
        plane = s1[pl.ds(w, HALF, stride=W_DEV), :]
        s2[pl.ds(w, 2 * BINS, stride=W_DEV), :] = plane.T * keep
    size = F_DEV * 2 * W_DEV
    for g in range(N_BIN):
        piece = s2[g * size:(g + 1) * size, :].astype(jnp.bfloat16)
        out_ref[g] = piece.reshape(F_DEV, 2 * W_DEV, HALF)


def transform(records, table, live, offsets=None):
    vmem = pl.BlockSpec(memory_space=pltpu.VMEM)
    hbm = pl.BlockSpec(memory_space=pltpu.HBM)
    smem = pl.BlockSpec(memory_space=pltpu.SMEM)
    out_shape = jax.ShapeDtypeStruct((N_BIN, F_DEV, 2 * W_DEV, HALF), jnp.bfloat16)
    plan_shapes = [jax.ShapeDtypeStruct((n,), jnp.int32) for n in (1, 2)]
    extra = () if offsets is None else (offsets,)
    return pl.pallas_call(
        functools.partial(transform_kernel, 1) if offsets is None else plan_kernel,
        out_shape=out_shape if offsets is None else [out_shape, *plan_shapes],
        in_specs=[smem] * len(extra) + [hbm, hbm, vmem],
        out_specs=vmem if offsets is None else [vmem, smem, smem],
        scratch_shapes=[
            pltpu.VMEM((HALF, W_DEV, SAMPLES), jnp.bfloat16),
            pltpu.VMEM((SAMPLES, 2 * BINS), jnp.bfloat16),
            pltpu.VMEM((HALF * W_DEV, 2 * BINS), jnp.float32),
            pltpu.VMEM((2 * BINS * W_DEV, HALF), jnp.float32),
            pltpu.SemaphoreType.DMA((HALF // STEP + 1,)),
        ],
        compiler_params=pltpu.CompilerParams(vmem_limit_bytes=LIMIT),
        cost_estimate=pl.CostEstimate(
            flops=2 * HALF * W_DEV * SAMPLES * 2 * BINS,
            bytes_accessed=HALF * W_DEV * SAMPLES * 2,
            transcendentals=0,
        ),
        name="transform",
    )(*extra, records, table, live)


K_ALL = N_BIN * 2 * W_DEV
OUT = jax.ShapeDtypeStruct((PAIRS, F_DEV, 2, BLOCK, BLOCK), jnp.bfloat16)


def rows_of(left, right, f):
    halves = [part[:, pl.ds(f, 1)].reshape(K_ALL, HALF) for part in (left, right)]
    return jnp.concatenate(halves, axis=1)


def left_of(mine):
    split = mine.reshape(N_BIN, 2, W_DEV, BLOCK)
    turned = jnp.concatenate([-split[:, 1:], split[:, :1]], axis=1)
    return jnp.concatenate([mine.T, turned.reshape(K_ALL, BLOCK).T], axis=0)


def product(left, theirs):
    both = jnp.dot(left, theirs, preferred_element_type=jnp.float32) * SCALE
    return both.reshape(2, BLOCK, BLOCK).astype(jnp.bfloat16)


def rounds_of(part, q_ref, left, near, far, out_hbm, stage, sems, f):
    stage[f] = product(left, rows_of(near, far, f))
    for copy in round_copies(part, q_ref, out_hbm, stage, sems, f):
        copy.start()


def round_copies(part, q_ref, out_hbm, stage, sems, f):
    columns = pl.ds(part * HALF, HALF)
    return [
        pltpu.make_async_copy(
            stage.at[f, :, :, pl.ds(n * HALF, HALF)],
            out_hbm.at[q_ref[n], f, :, :, columns],
            sems.at[n, f],
        )
        for n in range(2)
    ]


def first_kernel(q_ref, own1, own2, near, far, out_hbm, left_ref, own_stage, stage, own_sems, sems):
    def own_copy(f):
        return pltpu.make_async_copy(own_stage.at[f], out_hbm.at[0, f], own_sems.at[f])

    def step(f, carry):
        mine = rows_of(own1, own2, f)
        left = left_of(mine)
        left_ref[f] = left
        own_stage[f] = product(left, mine)
        own_copy(f).start()
        rounds_of(0, q_ref, left, near, far, out_hbm, stage, sems, f)
        return carry

    lax.fori_loop(0, F_DEV, step, 0)

    def finish(f, carry):
        own_copy(f).wait()
        for copy in round_copies(0, q_ref, out_hbm, stage, sems, f):
            copy.wait()
        return carry

    lax.fori_loop(0, F_DEV, finish, 0)


def first_pairs(pairings, *parts):
    vmem = pl.BlockSpec(memory_space=pltpu.VMEM)
    slots = pltpu.VMEM((F_DEV, 2, BLOCK, BLOCK), jnp.bfloat16)
    return pl.pallas_call(
        first_kernel,
        out_shape=[OUT, jax.ShapeDtypeStruct((F_DEV, 2 * BLOCK, K_ALL), jnp.bfloat16)],
        in_specs=[pl.BlockSpec(memory_space=pltpu.SMEM)] + [vmem] * 4,
        out_specs=[pl.BlockSpec(memory_space=pl.ANY), vmem],
        scratch_shapes=[
            slots,
            slots,
            pltpu.SemaphoreType.DMA((F_DEV,)),
            pltpu.SemaphoreType.DMA((2, F_DEV)),
        ],
        compiler_params=pltpu.CompilerParams(vmem_limit_bytes=16 << 20),
        cost_estimate=pl.CostEstimate(
            flops=2 * 2 * F_DEV * 2 * BLOCK * K_ALL * BLOCK,
            bytes_accessed=8 << 20,
            transcendentals=0,
        ),
        name="first_pairs",
    )(pairings, *parts)


def last_kernel(q_ref, left_ref, near, far, _, out_hbm, stage, sems):
    def step(f, carry):
        rounds_of(1, q_ref, left_ref[f], near, far, out_hbm, stage, sems, f)
        return carry

    lax.fori_loop(0, F_DEV, step, 0, unroll=2)

    def finish(f, carry):
        for copy in round_copies(1, q_ref, out_hbm, stage, sems, f):
            copy.wait()
        return carry

    lax.fori_loop(0, F_DEV, finish, 0)


def last_pairs(pairings, left, near, far, out):
    vmem = pl.BlockSpec(memory_space=pltpu.VMEM)
    hbm = pl.BlockSpec(memory_space=pl.ANY)
    return pl.pallas_call(
        last_kernel,
        out_shape=OUT,
        in_specs=[pl.BlockSpec(memory_space=pltpu.SMEM), vmem, vmem, vmem, hbm],
        out_specs=hbm,
        scratch_shapes=[
            pltpu.VMEM((F_DEV, 2, BLOCK, BLOCK), jnp.bfloat16),
            pltpu.SemaphoreType.DMA((2, F_DEV)),
        ],
        input_output_aliases={4: 0},
        compiler_params=pltpu.CompilerParams(vmem_limit_bytes=12 << 20),
        cost_estimate=pl.CostEstimate(
            flops=2 * F_DEV * 2 * BLOCK * K_ALL * BLOCK, bytes_accessed=5 << 20, transcendentals=0
        ),
        name="last_pairs",
    )(pairings, left, near, far, out)


def towards(value, offset):
    return lax.ppermute(
        value, "chan", [((a + offset) % N_CHAN, a) for a in range(N_CHAN)]
    )


def regroup(value):
    return lax.all_to_all(value, "bin", split_axis=0, concat_axis=0, tiled=True)


def rounds(k, own1, raw2, pairings):
    far1 = towards(own1, k)
    own2 = regroup(raw2)
    near1 = towards(own1, N_CHAN - 1)
    far2 = towards(own2, k)
    near2 = towards(own2, N_CHAN - 1)
    out, left = first_pairs(pairings, own1, own2, near1, far1)
    return last_pairs(pairings, left, near2, far2, out)


def body(records, live_traces, round_offsets):
    table = jnp.asarray(dft_table())
    live = live_traces.reshape(1, BLOCK)
    raw1, branch, pairings = transform(records, table, live, round_offsets)
    raw2 = transform(records, table, live)
    own1 = regroup(raw1)
    branches = [functools.partial(rounds, offset) for offset in range(1, N_CHAN - 1)]
    return lax.switch(branch[0], branches, own1, raw2, pairings)


def solution(mesh):
    in_specs = (P("chan", "bin", None), P("chan"), P())
    out_specs = P(None, "bin", None, "chan", None)
    return jax.shard_map(body, mesh=mesh, in_specs=in_specs, out_specs=out_specs, check_vma=False)
```

```python
import functools
import math

import numpy as np
import jax
import jax.numpy as jnp
from jax import lax
from jax.experimental import pallas as pl
from jax.experimental.pallas import tpu as pltpu
from jax.sharding import PartitionSpec as P

SAMPLES = 2048
BINS = 64
BAND_LO = 64
WINDOWS = 128
N_CHAN = 16
N_BIN = 8
EPS = 1e-06

BLOCK = 256
LANES = 128
STEP = 32
W_DEV = 16
F_DEV = 8
HALF = 128
PAIRS = 3
LIMIT = 60 * 1024 * 1024
SCALE = 1.0 / math.sqrt(WINDOWS)


def dft_table():
    samples = np.arange(SAMPLES, dtype=np.int64)
    freqs = BAND_LO + np.arange(BINS, dtype=np.int64)
    phase = samples[:, None] * freqs[None, :] % SAMPLES
    angle = phase.astype(np.float64) * (2.0 * math.pi / SAMPLES)
    both = np.stack([np.cos(angle), -np.sin(angle)], axis=-1) / math.sqrt(SAMPLES)
    return both.reshape(SAMPLES, 2 * BINS).astype(np.float32).astype(jnp.bfloat16)


def plan_kernel(offsets_ref, x_hbm, t_hbm, live_ref, out_ref, branch_ref, pairings_ref, *scratch):
    last_first = offsets_ref[0] == N_CHAN - 1
    branch_ref[0] = jnp.where(last_first, offsets_ref[1], offsets_ref[0]) - 1
    near = jnp.where(last_first, 1, 2)
    pairings_ref[0] = near
    pairings_ref[1] = PAIRS - near
    transform_kernel(0, x_hbm, t_hbm, live_ref, out_ref, *scratch)


def transform_kernel(part, x_hbm, t_hbm, live_ref, out_ref, xb, table, s1, s2, sems):
    steps = HALF // STEP
    rows = STEP * W_DEV

    def load(b):
        return pltpu.make_async_copy(
            x_hbm.at[pl.ds(part * HALF + b * STEP, STEP)],
            xb.at[pl.ds(b * STEP, STEP)],
            sems.at[b],
        )

    load_table = pltpu.make_async_copy(t_hbm, table, sems.at[steps])
    load(0).start()
    load_table.start()
    for b in range(1, steps):
        load(b).start()
    load_table.wait()

    def step(b, carry):
        load(b).wait()
        x = xb[pl.ds(b * STEP, STEP)].reshape(rows, SAMPLES)
        res = jnp.dot(x, table[...], preferred_element_type=jnp.float32)
        acc = None
        for j in range(SAMPLES // LANES):
            piece = x[:, j * LANES:(j + 1) * LANES].astype(jnp.float32)
            acc = piece * piece if acc is None else acc + piece * piece
        power = jnp.sum(acc, axis=-1, keepdims=True) * (1.0 / SAMPLES)
        s1[pl.ds(pl.multiple_of(b * rows, rows), rows), :] = res * lax.rsqrt(power + EPS)
        return carry

    lax.fori_loop(0, steps, step, 0)
    keep = live_ref[:, part * HALF:(part + 1) * HALF].astype(jnp.float32)
    for w in range(W_DEV):
        plane = s1[pl.ds(w, HALF, stride=W_DEV), :]
        s2[pl.ds(w, 2 * BINS, stride=W_DEV), :] = plane.T * keep
    size = F_DEV * 2 * W_DEV
    for g in range(N_BIN):
        piece = s2[g * size:(g + 1) * size, :].astype(jnp.bfloat16)
        out_ref[g] = piece.reshape(F_DEV, 2 * W_DEV, HALF)


def transform(records, table, live, offsets=None):
    vmem = pl.BlockSpec(memory_space=pltpu.VMEM)
    hbm = pl.BlockSpec(memory_space=pltpu.HBM)
    smem = pl.BlockSpec(memory_space=pltpu.SMEM)
    out_shape = jax.ShapeDtypeStruct((N_BIN, F_DEV, 2 * W_DEV, HALF), jnp.bfloat16)
    plan_shapes = [jax.ShapeDtypeStruct((n,), jnp.int32) for n in (1, 2)]
    extra = () if offsets is None else (offsets,)
    return pl.pallas_call(
        functools.partial(transform_kernel, 1) if offsets is None else plan_kernel,
        out_shape=out_shape if offsets is None else [out_shape, *plan_shapes],
        in_specs=[smem] * len(extra) + [hbm, hbm, vmem],
        out_specs=vmem if offsets is None else [vmem, smem, smem],
        scratch_shapes=[
            pltpu.VMEM((HALF, W_DEV, SAMPLES), jnp.bfloat16),
            pltpu.VMEM((SAMPLES, 2 * BINS), jnp.bfloat16),
            pltpu.VMEM((HALF * W_DEV, 2 * BINS), jnp.float32),
            pltpu.VMEM((2 * BINS * W_DEV, HALF), jnp.float32),
            pltpu.SemaphoreType.DMA((HALF // STEP + 1,)),
        ],
        compiler_params=pltpu.CompilerParams(vmem_limit_bytes=LIMIT),
        cost_estimate=pl.CostEstimate(
            flops=2 * HALF * W_DEV * SAMPLES * 2 * BINS,
            bytes_accessed=HALF * W_DEV * SAMPLES * 2,
            transcendentals=0,
        ),
        name="transform",
    )(*extra, records, table, live)


K_ALL = N_BIN * 2 * W_DEV
OUT = jax.ShapeDtypeStruct((PAIRS, F_DEV, 2, BLOCK, BLOCK), jnp.bfloat16)


def rows_of(left, right, f):
    halves = [part[:, pl.ds(f, 1)].reshape(K_ALL, HALF) for part in (left, right)]
    return jnp.concatenate(halves, axis=1)


def left_of(mine):
    split = mine.reshape(N_BIN, 2, W_DEV, BLOCK)
    turned = jnp.concatenate([-split[:, 1:], split[:, :1]], axis=1)
    return jnp.concatenate([mine.T, turned.reshape(K_ALL, BLOCK).T], axis=0)


def product(left, theirs):
    both = jnp.dot(left, theirs, preferred_element_type=jnp.float32) * SCALE
    return both.reshape(2, BLOCK, BLOCK).astype(jnp.bfloat16)


def rounds_of(part, q_ref, left, near, far, out_hbm, stage, sems, f):
    stage[f] = product(left, rows_of(near, far, f))
    for copy in round_copies(part, q_ref, out_hbm, stage, sems, f):
        copy.start()


def round_copies(part, q_ref, out_hbm, stage, sems, f):
    columns = pl.ds(part * HALF, HALF)
    return [
        pltpu.make_async_copy(
            stage.at[f, :, :, pl.ds(n * HALF, HALF)],
            out_hbm.at[q_ref[n], f, :, :, columns],
            sems.at[n, f],
        )
        for n in range(2)
    ]


def first_kernel(q_ref, own1, own2, near, far, out_hbm, left_ref, own_stage, stage, own_sems, sems):
    def own_copy(f):
        return pltpu.make_async_copy(own_stage.at[f], out_hbm.at[0, f], own_sems.at[f])

    def step(f, carry):
        mine = rows_of(own1, own2, f)
        left = left_of(mine)
        left_ref[f] = left
        own_stage[f] = product(left, mine)
        own_copy(f).start()
        rounds_of(0, q_ref, left, near, far, out_hbm, stage, sems, f)
        return carry

    lax.fori_loop(0, F_DEV, step, 0)

    def finish(f, carry):
        own_copy(f).wait()
        for copy in round_copies(0, q_ref, out_hbm, stage, sems, f):
            copy.wait()
        return carry

    lax.fori_loop(0, F_DEV, finish, 0)


def first_pairs(pairings, *parts):
    vmem = pl.BlockSpec(memory_space=pltpu.VMEM)
    slots = pltpu.VMEM((F_DEV, 2, BLOCK, BLOCK), jnp.bfloat16)
    return pl.pallas_call(
        first_kernel,
        out_shape=[OUT, jax.ShapeDtypeStruct((F_DEV, 2 * BLOCK, K_ALL), jnp.bfloat16)],
        in_specs=[pl.BlockSpec(memory_space=pltpu.SMEM)] + [vmem] * 4,
        out_specs=[pl.BlockSpec(memory_space=pl.ANY), vmem],
        scratch_shapes=[
            slots,
            slots,
            pltpu.SemaphoreType.DMA((F_DEV,)),
            pltpu.SemaphoreType.DMA((2, F_DEV)),
        ],
        compiler_params=pltpu.CompilerParams(vmem_limit_bytes=16 << 20),
        cost_estimate=pl.CostEstimate(
            flops=2 * 2 * F_DEV * 2 * BLOCK * K_ALL * BLOCK,
            bytes_accessed=8 << 20,
            transcendentals=0,
        ),
        name="first_pairs",
    )(pairings, *parts)


def last_kernel(q_ref, left_ref, near, far, _, out_hbm, stage, sems):
    def step(f, carry):
        rounds_of(1, q_ref, left_ref[f], near, far, out_hbm, stage, sems, f)
        return carry

    lax.fori_loop(0, F_DEV, step, 0, unroll=2)

    def finish(f, carry):
        for copy in round_copies(1, q_ref, out_hbm, stage, sems, f):
            copy.wait()
        return carry

    lax.fori_loop(0, F_DEV, finish, 0)


def last_pairs(pairings, left, near, far, out):
    vmem = pl.BlockSpec(memory_space=pltpu.VMEM)
    hbm = pl.BlockSpec(memory_space=pl.ANY)
    return pl.pallas_call(
        last_kernel,
        out_shape=OUT,
        in_specs=[pl.BlockSpec(memory_space=pltpu.SMEM), vmem, vmem, vmem, hbm],
        out_specs=hbm,
        scratch_shapes=[
            pltpu.VMEM((F_DEV, 2, BLOCK, BLOCK), jnp.bfloat16),
            pltpu.SemaphoreType.DMA((2, F_DEV)),
        ],
        input_output_aliases={4: 0},
        compiler_params=pltpu.CompilerParams(vmem_limit_bytes=12 << 20),
        cost_estimate=pl.CostEstimate(
            flops=2 * F_DEV * 2 * BLOCK * K_ALL * BLOCK, bytes_accessed=5 << 20, transcendentals=0
        ),
        name="last_pairs",
    )(pairings, left, near, far, out)


def towards(value, offset):
    return lax.ppermute(
        value, "chan", [((a + offset) % N_CHAN, a) for a in range(N_CHAN)]
    )


def regroup(value):
    return lax.all_to_all(value, "bin", split_axis=0, concat_axis=0, tiled=True)


def rounds(k, own1, raw2, pairings):
    far1 = towards(own1, k)
    own2 = regroup(raw2)
    near1 = towards(own1, N_CHAN - 1)
    far2 = towards(own2, k)
    near2 = towards(own2, N_CHAN - 1)
    out, left = first_pairs(pairings, own1, own2, near1, far1)
    return last_pairs(pairings, left, near2, far2, out)


def body(records, live_traces, round_offsets):
    table = jnp.asarray(dft_table())
    live = live_traces.reshape(1, BLOCK)
    raw1, branch, pairings = transform(records, table, live, round_offsets)
    raw2 = transform(records, table, live)
    own1 = regroup(raw1)
    branches = [functools.partial(rounds, offset) for offset in range(1, N_CHAN - 1)]
    return lax.switch(branch[0], branches, own1, raw2, pairings)


def solution(mesh):
    in_specs = (P("chan", "bin", None), P("chan"), P())
    out_specs = P(None, "bin", None, "chan", None)
    return jax.shard_map(body, mesh=mesh, in_specs=in_specs, out_specs=out_specs, check_vma=False)
```
